32 devices in a mesh: row: 8 (over y, x, core), col: 4 (over z).
Axes of the slice: x: 2, y: 2, z: 4, core: 2. Of those that a mesh axis runs over, the one named last changes fastest.
Arguments:
- features: float32 [8192, 256], P(('row', 'col')), may hold values from -6 to 6
- new_features: float32 [2048, 256], P(('row', 'col')), may hold values from -6 to 6
- lengths: int32 [8192], P(('row', 'col')), may hold values from 1 to 64
- targets: float32 [8192, 64], P(('row', 'col')), may hold values from -6 to 6
- prior_train: float32 [8192, 256], P(('row', 'col')), may hold values from -6 to 6
- noise_draw: float32 [8192, 256], P(('row', 'col')), may hold values from -6 to 6
- prior_new: float32 [2048, 256], P(('row', 'col')), may hold values from -6 to 6
- time_kernel: float32 [64, 64], replicated, may hold values from -16 to 16.5, as said below
- noise_var: float32 [64], replicated, may hold values from 0.05 to 0.5
Outputs:
- residual: float32 [8192, 256], P(('row', 'col'))
- predicted: float32 [2048, 256], P(('row', 'col'))
The draws below stay inside these ranges and needn't reach their ends.
Inputs may be any that keep to these rules, and one draw needn't show every extreme that they name: `time_kernel`: symmetric positive definite.
All inputs are finite; a program needn't handle non-finite values.
Results may differ from the reference program's by a relative error of at most 0.00022.
Values sent between devices are 32-bit elements; how exact they have to be, the bound alone decides.
A program may use at most 128 MiB of HBM per device.

```python
import math
import jax
import jax.numpy as jnp
from jax import lax

FEATURES = 256
CHECKPOINTS = 64
SAMPLES = 4
ITERS = 2
ITEMS = 8192
NEW_ITEMS = 2048
N_ROW = 8


def draw_time_kernel(key, part):
    first = jax.random.fold_in(jax.random.fold_in(key, 17), 0)
    base = jnp.clip(jax.random.normal(first, (CHECKPOINTS, CHECKPOINTS), jnp.float32), -4.0, 4.0)
    gram = jnp.dot(base, base.T, precision=lax.Precision.HIGHEST) / CHECKPOINTS
    return gram + 0.5 * jnp.eye(CHECKPOINTS, dtype=jnp.float32)


def plant(values, rng, smallest, high):
    longest = values.shape.index(max(values.shape))
    spots = []
    for shift in (0, 1):
        where = [jax.random.randint(jax.random.fold_in(rng, axis), (), 0, length) for axis, length in enumerate(values.shape)]
        where[longest] = (where[longest] + shift) % values.shape[longest]
        spots.append(tuple(where))
    return values.at[spots[0]].set(smallest).at[spots[1]].set(high)


def shard_levels(key, dims, cuts, least, high):
    level = 1.0
    for axis_at, shards_of in cuts:
        steps = jax.random.uniform(jax.random.fold_in(jax.random.fold_in(key, 6), axis_at), (shards_of,), jnp.float32, least / len(cuts), high / len(cuts))
        level = level * jnp.repeat(jnp.exp(steps), dims[axis_at] // shards_of).reshape((-1,) + (1,) * (len(dims) - 1 - axis_at))
    return level


def noise(stream_key, extent, deviation, reach, pieces=(), kind=jnp.bfloat16):
    gain = shard_levels(stream_key, extent, pieces, -0.22, 0.18) if pieces else 1.0
    values = jax.random.normal(stream_key, extent, jnp.float32) * deviation * gain
    return jnp.minimum(jnp.maximum(values, -reach), reach).astype(kind)


def setup_inputs(seed: int = 0) -> dict:
    streams_of = jax.random.split(jax.random.key(seed), 10)
    return {
        "features": noise(streams_of[0], (ITEMS, FEATURES), 1.0, 6.0, ((0, 32),), jnp.float32),
        "new_features": noise(streams_of[1], (NEW_ITEMS, FEATURES), 1.0, 6.0, ((0, 32),), jnp.float32),
        "lengths": plant(jax.random.randint(streams_of[2], (ITEMS,), 1, CHECKPOINTS + 1), jax.random.fold_in(streams_of[2], 1), 1, CHECKPOINTS).astype(jnp.int32),
        "targets": noise(streams_of[3], (ITEMS, CHECKPOINTS), 1.0, 6.0, ((0, 32),), jnp.float32),
        "prior_train": noise(streams_of[4], (ITEMS, SAMPLES * CHECKPOINTS), 1.0, 6.0, ((0, 32),), jnp.float32),
        "noise_draw": noise(streams_of[5], (ITEMS, SAMPLES * CHECKPOINTS), 1.0, 6.0, ((0, 32),), jnp.float32),
        "prior_new": noise(streams_of[6], (NEW_ITEMS, SAMPLES * CHECKPOINTS), 1.0, 6.0, ((0, 32),), jnp.float32),
        "time_kernel": draw_time_kernel(jax.random.fold_in(streams_of[9], 71), 0),
        "noise_var": jnp.clip(jnp.exp(jax.random.uniform(streams_of[8], (CHECKPOINTS,), jnp.float32, math.log(0.05), math.log(0.5))), 0.05, 0.5),
    }


def unit_rows(values):
    return values / jnp.sqrt(lax.optimization_barrier(jnp.sum(values * values, axis=1, keepdims=True)) + 1e-06)

def kernel(left, right):
    inner = lax.dot_general(left, right, (((1,), (1,)), ((), ())), precision=lax.Precision.HIGHEST)
    return inner + inner * inner * inner

def kernel_apply(left, right, values):
    blocks = left.reshape(N_ROW, -1, left.shape[1])

    def one_block(block):
        return jnp.dot(kernel(block, right), values, precision=lax.Precision.HIGHEST)
    return lax.map(one_block, blocks).reshape(-1, values.shape[1])

def reference(features, new_features, lengths, targets, prior_train, noise_draw, prior_new, time_kernel, noise_var):
    normed = unit_rows(features)
    normed_new = unit_rows(new_features)
    mixing = jnp.kron(jnp.eye(SAMPLES, dtype=time_kernel.dtype), time_kernel)
    position = jnp.arange(SAMPLES * CHECKPOINTS, dtype=jnp.int32) % CHECKPOINTS
    mask = (position[None, :] < lengths[:, None]).astype(targets.dtype)
    noise_cols = jnp.tile(noise_var, SAMPLES)
    rhs = mask * (jnp.tile(targets, (1, SAMPLES)) - prior_train - jnp.sqrt(noise_cols) * noise_draw)

    def operate(direction):
        mixed = jnp.dot(direction, mixing, precision=lax.Precision.HIGHEST)
        return mask * kernel_apply(normed, normed, mixed) + noise_cols * direction

    def per_sample(first, second):
        return lax.optimization_barrier(jnp.sum((first * second).reshape(first.shape[0], SAMPLES, CHECKPOINTS), axis=(0, 2)))
    solution = jnp.zeros_like(rhs)
    residual = rhs
    direction = rhs
    norm_now = per_sample(residual, residual)
    for step in range(ITERS):
        image = operate(direction)
        alpha = jnp.repeat(norm_now / per_sample(direction, image), CHECKPOINTS)
        solution = solution + alpha * direction
        residual = residual - alpha * image
        if step + 1 < ITERS:
            norm_next = per_sample(residual, residual)
            direction = residual + jnp.repeat(norm_next / norm_now, CHECKPOINTS) * direction
            norm_now = norm_next
    mixed_solution = jnp.dot(solution, mixing, precision=lax.Precision.HIGHEST)
    predicted = prior_new + kernel_apply(normed_new, normed, mixed_solution)
    return (residual, predicted)
```

```python
import functools

import jax
import jax.numpy as jnp
from jax import lax
from jax.experimental import pallas as pl
from jax.experimental.pallas import tpu as pltpu
from jax.sharding import PartitionSpec as P

MESH = pl.DeviceIdType.MESH
F32 = jnp.float32
BF16 = jnp.bfloat16
HIGHEST = lax.Precision.HIGHEST


def split(values):
    high = values.astype(BF16)
    return high, (values - high.astype(F32)).astype(BF16)


def dot3(left, right, dims):
    def one(a, b):
        return lax.dot_general(a, b, (dims, ((), ())), preferred_element_type=F32)

    return one(left[0], right[0]) + (one(left[0], right[1]) + one(left[1], right[0]))


NT = ((1,), (1,))
NN = ((1,), (0,))


def dot_full(a, b, dims=NN):
    return lax.dot_general(a, b, (dims, ((), ())), precision=HIGHEST, preferred_element_type=F32)


def unit_rows(values):
    return values / jnp.sqrt(jnp.sum(values * values, axis=1, keepdims=True) + 1e-06)


def cubic(inner):
    return inner + inner * inner * inner


def body(
    rows,
    cols,
    keep,
    feat,
    feat_new,
    lengths,
    targets,
    prior,
    draw,
    prior_new,
    time_kernel,
    noise_var,
    out_res,
    out_pred,
    ncol,
    nrow,
    nnew,
    v0,
    v1,
    nch,
    ncl,
    kh,
    kl,
    vh,
    vl,
    xacc,
    got,
    xgot,
    rhs_ref,
    mask_ref,
    image_ref,
    mix_ref,
    dots_row,
    dots_col,
    n_send,
    n_recv,
    v_send,
    v_recv,
    z_send,
    z_recv,
    w_send,
    w_recv,
    rs_send,
    rs_recv,
    xs_send,
    xs_recv,
    dr_send,
    dr_recv,
    dc_send,
    dc_recv,
):
    block = feat.shape[0]
    fresh = feat_new.shape[0]
    width = prior.shape[1]
    points = time_kernel.shape[0]
    half = rows // 2
    r = lax.axis_index("row")
    c = lax.axis_index("col")
    pair, core = r // 2, lax.rem(r, 2)
    mate = 2 * pair + 1 - core

    def loop(low, high, step):
        def run(k, carry):
            step(k)
            return carry

        lax.fori_loop(low, high, run, 0)

    def remote(src, dst, send, recv, row, col):
        return pltpu.make_async_remote_copy(
            src_ref=src,
            dst_ref=dst,
            send_sem=send,
            recv_sem=recv,
            device_id=(row, col),
            device_id_type=MESH,
        )

    barrier = pltpu.get_barrier_semaphore()

    def greet_row(k):
        pl.semaphore_signal(barrier, inc=1, device_id=(lax.rem(r + k, rows), c), device_id_type=MESH)

    def greet_col(k):
        pl.semaphore_signal(barrier, inc=1, device_id=(r, lax.rem(c + k, cols)), device_id_type=MESH)

    loop(1, rows, greet_row)
    loop(1, cols, greet_col)

    normed = unit_rows(feat[...])
    ncol[r] = normed
    nrow[c] = normed
    nnew[c] = unit_rows(feat_new[...])

    pl.semaphore_wait(barrier, rows + cols - 2)

    def spread_start(buf, send, recv):
        def to_pair(k):
            there = 2 * lax.rem(pair + k, half) + core
            remote(buf.at[r], buf.at[r], send.at[k], recv.at[r], there, c).start()

        loop(1, half, to_pair)
        remote(buf.at[r], buf.at[r], send.at[0], recv.at[r], mate, c).start()

    def like(k):
        return 2 * lax.rem(pair + half - k, half) + core

    def unlike(k):
        return 2 * lax.rem(pair + half - k, half) + 1 - core

    def spread_forward(buf, send, recv, use):
        def one(k):
            j = like(k)
            fwd = remote(buf.at[j], buf.at[j], send.at[half - 1 + k], recv.at[j], mate, c)
            fwd.wait_recv()
            fwd.start()
            use(j)

        loop(1, half, one)

    def spread_rest(buf, send, recv, use):
        def one(k):
            j = unlike(k)
            remote(buf.at[j], buf.at[j], send.at[0], recv.at[j], mate, c).wait_recv()
            use(j)

        loop(0, half, one)

    def spread_end(buf, send, recv):
        def one(k):
            remote(buf.at[r], buf.at[r], send.at[k], recv.at[r], mate, c).wait_send()

        loop(0, rows - 1, one)

    def line_start(src_of, dst, send, recv):
        def one(k):
            there = lax.rem(c + k, cols)
            remote(src_of(there), dst.at[c], send.at[k], recv.at[c], r, there).start()

        loop(1, cols, one)

    def line_wait(dst, send, recv, k):
        src = lax.rem(c + cols - k, cols)
        remote(dst.at[src], dst.at[src], send.at[k], recv.at[src], r, lax.rem(c + k, cols)).wait_recv()
        return src

    def line_end(dst, send, recv):
        def one(k):
            there = lax.rem(c + k, cols)
            remote(dst.at[c], dst.at[c], send.at[k], recv.at[c], r, there).wait_send()

        loop(1, cols, one)

    line_start(lambda there: nrow.at[c], nrow, z_send, z_recv)
    spread_start(ncol, n_send, n_recv)
    line_start(lambda there: nnew.at[c], nnew, w_send, w_recv)

    lane = lax.broadcasted_iota(jnp.int32, (points, width), 1)
    line = lax.broadcasted_iota(jnp.int32, (points, width), 0)
    repeat = (lax.rem(lane, points) == line).astype(F32)
    wide_row = lax.broadcasted_iota(jnp.int32, (width, width), 0) // points
    wide_col = lax.broadcasted_iota(jnp.int32, (width, width), 1) // points
    same = (wide_row == wide_col).astype(F32)
    mix_ref[...] = same * dot_full(repeat, dot_full(time_kernel[...], repeat), ((0,), (0,)))
    noise_cols = dot_full(jnp.broadcast_to(noise_var[...], (8, points)), repeat)[0:1]
    place = lax.rem(lax.broadcasted_iota(jnp.int32, (block, width), 1), points)
    mask = (place < lengths[...]).astype(F32)
    mask_ref[...] = mask
    rhs = mask * (dot_full(targets[...], repeat) - prior[...] - jnp.sqrt(noise_cols) * draw[...])
    rhs_ref[...] = rhs
    v0[r] = dot_full(rhs, mix_ref[...])
    spread_start(v0, v_send.at[0], v_recv.at[0])

    def keep_split(j):
        if keep:
            high, low = split(ncol[j])
            nch[j] = high
            ncl[j] = low

    def right(j):
        return (nch[j], ncl[j]) if keep else split(ncol[j])

    keep_split(r)
    spread_forward(ncol, n_send, n_recv, keep_split)
    spread_rest(ncol, n_send, n_recv, keep_split)

    def build(at):
        left = split(nrow[at])
        for j in range(rows):
            tile = cubic(dot3(left, right(j), NT))
            high, low = split(tile)
            kh[at, :, j * block : (j + 1) * block] = high
            kl[at, :, j * block : (j + 1) * block] = low

    build(c)

    def keep_values(j):
        high, low = split(v0[j])
        here = pl.ds(pl.multiple_of(j * block, block), block)
        vh[here, :] = high
        vl[here, :] = low

    keep_values(r)
    spread_forward(v0, v_send.at[0], v_recv.at[0], keep_values)

    def build_next(k):
        build(line_wait(nrow, z_send, z_recv, k))

    loop(1, cols, build_next)
    spread_rest(v0, v_send.at[0], v_recv.at[0], keep_values)

    def apply(step):
        def one(k):
            there = lax.rem(c + k, cols)
            acc[there] = dot3((kh[there], kl[there]), (vh[...], vl[...]), NN)

            @pl.when(k < cols)
            def _():
                remote(
                    acc.at[there], got.at[step, c], rs_send.at[step, k], rs_recv.at[step, c], r, there
                ).start()

        loop(1, cols + 1, one)

    def cross(step):
        left = split(nnew[...].reshape(cols * fresh, nnew.shape[2]))
        xacc[step] = jnp.zeros(xacc.shape[1:], F32)

        def one(j):
            tile = split(cubic(dot3(left, right(j), NT)))
            here = pl.ds(pl.multiple_of(j * block, block), block)
            part = dot3(tile, (vh[here, :], vl[here, :]), NN)
            xacc[step] += part.reshape(cols, fresh, width)

        loop(0, rows, one)
        line_start(lambda there: xacc.at[step, there], xgot.at[step], xs_send.at[step], xs_recv.at[step])

    def reduced(dst, own, send, recv):
        def wait(k):
            line_wait(dst, send, recv, k)

        loop(1, cols, wait)
        dst[c] = own
        return jnp.sum(dst[...], axis=0)

    def total_start(step):
        def one(k):
            there = lax.rem(r + k, rows)
            remote(
                dots_row.at[step, r], dots_row.at[step, r], dr_send.at[step, k], dr_recv.at[step, r], there, c
            ).start()

        loop(1, rows, one)

    def total_middle(step):
        def one(k):
            j = lax.rem(r + rows - k, rows)
            remote(
                dots_row.at[step, j], dots_row.at[step, j], dr_send.at[step, k], dr_recv.at[step, j], mate, c
            ).wait_recv()

        loop(1, rows, one)
        dots_col[step, c] = jnp.sum(dots_row[step], axis=0)
        line_start(lambda there: dots_col.at[step, c], dots_col.at[step], dc_send.at[step], dc_recv.at[step])

    def total_end(step):
        def one(k):
            line_wait(dots_col.at[step], dc_send.at[step], dc_recv.at[step], k)

        loop(1, cols, one)
        return dot_full(jnp.sum(dots_col[step], axis=0), same)

    def total_close(step):
        def one(k):
            remote(
                dots_row.at[step, r], dots_row.at[step, r], dr_send.at[step, k], dr_recv.at[step, r], mate, c
            ).wait_send()

        loop(1, rows, one)
        line_end(dots_col.at[step], dc_send.at[step], dc_recv.at[step])

    def column_sums(*values):
        sums = [jnp.sum(v, axis=0, keepdims=True) for v in values]
        return jnp.concatenate(sums + [jnp.zeros((8 - len(sums), width), F32)], axis=0)

    acc = nrow
    line_end(nrow, z_send, z_recv)
    apply(0)

    def wait_new(k):
        line_wait(nnew, w_send, w_recv, k)

    loop(1, cols, wait_new)
    cross(0)
    image0 = mask_ref[...] * reduced(got.at[0], acc[c], rs_send.at[0], rs_recv.at[0]) + noise_cols * rhs_ref[...]
    image_ref[...] = image0
    dots_row[0, r] = column_sums(rhs_ref[...] * rhs_ref[...], rhs_ref[...] * image0)
    total_start(0)
    v1[r] = dot_full(image0, mix_ref[...])
    spread_start(v1, v_send.at[1], v_recv.at[1])
    total_middle(0)
    sums0 = total_end(0)
    alpha0 = sums0[0:1] / sums0[1:2]

    def keep_next(j):
        high, low = split(v0[j] - alpha0 * v1[j])
        here = pl.ds(pl.multiple_of(j * block, block), block)
        vh[here, :] = high
        vl[here, :] = low

    keep_next(r)
    spread_forward(v1, v_send.at[1], v_recv.at[1], keep_next)

    def free_acc(k):
        there = lax.rem(c + k, cols)
        remote(acc.at[there], got.at[0, c], rs_send.at[0, k], rs_recv.at[0, c], r, there).wait_send()

    loop(1, cols, free_acc)
    spread_rest(v1, v_send.at[1], v_recv.at[1], keep_next)

    apply(1)
    cross(1)
    residual = rhs_ref[...] - alpha0 * image_ref[...]
    image1 = mask_ref[...] * reduced(got.at[1], acc[c], rs_send.at[1], rs_recv.at[1]) + noise_cols * residual
    dots_row[1, r] = column_sums(
        residual * residual, residual * image1, residual * image_ref[...] + rhs_ref[...] * image1
    )
    total_start(1)
    total_middle(1)
    sums1 = total_end(1)
    ratio = sums1[0:1] / sums0[0:1]
    alpha1 = sums1[0:1] / (sums1[1:2] + ratio * (sums1[2:3] + ratio * sums0[1:2]))
    out_res[...] = residual - alpha1 * (image1 + ratio * image_ref[...])
    first = reduced(xgot.at[0], xacc[0, c], xs_send.at[0], xs_recv.at[0])
    second = reduced(xgot.at[1], xacc[1, c], xs_send.at[1], xs_recv.at[1])
    out_pred[...] = prior_new[...] + (alpha0 + alpha1 * ratio) * first + alpha1 * second

    spread_end(ncol, n_send, n_recv)
    line_end(nnew, w_send, w_recv)

    def free_last(k):
        there = lax.rem(c + k, cols)
        remote(acc.at[there], got.at[1, c], rs_send.at[1, k], rs_recv.at[1, c], r, there).wait_send()

    loop(1, cols, free_last)
    for step, buf in ((0, v0), (1, v1)):
        spread_end(buf, v_send.at[step], v_recv.at[step])
        line_end(xgot.at[step], xs_send.at[step], xs_recv.at[step])
        total_close(step)


def shards(rows, cols, features, new_features, lengths, targets, prior_train, noise_draw, prior_new, time_kernel, noise_var):
    block, depth = features.shape
    fresh = new_features.shape[0]
    width = prior_train.shape[1]
    vmem = pl.BlockSpec(memory_space=pltpu.VMEM)
    dma = pltpu.SemaphoreType.DMA
    assert depth == width
    keep = 4 * rows * cols * block * block <= 2**24
    kept = (rows, block, depth) if keep else (1, 16, depth)
    flops = 2 * 3 * block * cols * block * rows * (depth + 2 * width)
    return pl.pallas_call(
        functools.partial(body, rows, cols, keep),
        out_shape=(
            jax.ShapeDtypeStruct((block, width), F32),
            jax.ShapeDtypeStruct((fresh, width), F32),
        ),
        in_specs=[vmem] * 9,
        out_specs=(vmem, vmem),
        scratch_shapes=[
            pltpu.VMEM((rows, block, depth), F32),
            pltpu.VMEM((cols, block, depth), F32),
            pltpu.VMEM((cols, fresh, depth), F32),
            pltpu.VMEM((rows, block, width), F32),
            pltpu.VMEM((rows, block, width), F32),
            pltpu.VMEM(kept, BF16),
            pltpu.VMEM(kept, BF16),
            pltpu.VMEM((cols, block, rows * block), BF16),
            pltpu.VMEM((cols, block, rows * block), BF16),
            pltpu.VMEM((rows * block, width), BF16),
            pltpu.VMEM((rows * block, width), BF16),
            pltpu.VMEM((2, cols, fresh, width), F32),
            pltpu.VMEM((2, cols, block, width), F32),
            pltpu.VMEM((2, cols, fresh, width), F32),
            pltpu.VMEM((block, width), F32),
            pltpu.VMEM((block, width), F32),
            pltpu.VMEM((block, width), F32),
            pltpu.VMEM((width, width), F32),
            pltpu.VMEM((2, rows, 8, width), F32),
            pltpu.VMEM((2, cols, 8, width), F32),
            dma((rows,)),
            dma((rows,)),
            dma((2, rows)),
            dma((2, rows)),
            dma((cols,)),
            dma((cols,)),
            dma((cols,)),
            dma((cols,)),
            dma((2, cols)),
            dma((2, cols)),
            dma((2, cols)),
            dma((2, cols)),
            dma((2, rows)),
            dma((2, rows)),
            dma((2, cols)),
            dma((2, cols)),
        ],
        compiler_params=pltpu.CompilerParams(
            collective_id=0, has_side_effects=True, vmem_limit_bytes=63 * 2**20
        ),
        cost_estimate=pl.CostEstimate(flops=flops, bytes_accessed=8 * block * width * 4, transcendentals=0),
    )(
        features,
        new_features,
        lengths.reshape(block, 1),
        targets,
        prior_train,
        noise_draw,
        prior_new,
        time_kernel,
        noise_var.reshape(1, -1),
    )


def solution(mesh):
    both = ("row", "col")
    return jax.shard_map(
        functools.partial(shards, mesh.shape["row"], mesh.shape["col"]),
        mesh=mesh,
        in_specs=(
            P(both, None),
            P(both, None),
            P(both),
            P(both, None),
            P(both, None),
            P(both, None),
            P(both, None),
            P(),
            P(),
        ),
        out_specs=(P(both, None), P(both, None)),
        check_vma=False,
    )
```

```python
import functools

import jax
import jax.numpy as jnp
from jax import lax
from jax.experimental import pallas as pl
from jax.experimental.pallas import tpu as pltpu
from jax.sharding import PartitionSpec as P

MESH = pl.DeviceIdType.MESH
F32 = jnp.float32
BF16 = jnp.bfloat16
HIGHEST = lax.Precision.HIGHEST


def split(values):
    high = values.astype(BF16)
    return high, (values - high.astype(F32)).astype(BF16)


def dot3(left, right, dims):
    def one(a, b):
        return lax.dot_general(a, b, (dims, ((), ())), preferred_element_type=F32)

    return one(left[0], right[0]) + (one(left[0], right[1]) + one(left[1], right[0]))


NT = ((1,), (1,))
NN = ((1,), (0,))


def dot_full(a, b, dims=NN):
    return lax.dot_general(a, b, (dims, ((), ())), precision=HIGHEST, preferred_element_type=F32)


def unit_rows(values):
    return values / jnp.sqrt(jnp.sum(values * values, axis=1, keepdims=True) + 1e-06)


def cubic(inner):
    return inner + inner * inner * inner


def body(
    rows,
    cols,
    keep,
    feat,
    feat_new,
    lengths,
    targets,
    prior,
    draw,
    prior_new,
    time_kernel,
    noise_var,
    out_res,
    out_pred,
    ncol,
    nrow,
    nnew,
    v0,
    v1,
    nch,
    ncl,
    kh,
    kl,
    vh,
    vl,
    xacc,
    got,
    xgot,
    rhs_ref,
    mask_ref,
    image_ref,
    mix_ref,
    dots_row,
    dots_col,
    n_send,
    n_recv,
    v_send,
    v_recv,
    z_send,
    z_recv,
    w_send,
    w_recv,
    rs_send,
    rs_recv,
    xs_send,
    xs_recv,
    dr_send,
    dr_recv,
    dc_send,
    dc_recv,
):
    block = feat.shape[0]
    fresh = feat_new.shape[0]
    width = prior.shape[1]
    points = time_kernel.shape[0]
    half = rows // 2
    r = lax.axis_index("row")
    c = lax.axis_index("col")
    pair, core = r // 2, lax.rem(r, 2)
    mate = 2 * pair + 1 - core

    def loop(low, high, step):
        def run(k, carry):
            step(k)
            return carry

        lax.fori_loop(low, high, run, 0)

    def remote(src, dst, send, recv, row, col):
        return pltpu.make_async_remote_copy(
            src_ref=src,
            dst_ref=dst,
            send_sem=send,
            recv_sem=recv,
            device_id=(row, col),
            device_id_type=MESH,
        )

    barrier = pltpu.get_barrier_semaphore()

    def greet_row(k):
        pl.semaphore_signal(barrier, inc=1, device_id=(lax.rem(r + k, rows), c), device_id_type=MESH)

    def greet_col(k):
        pl.semaphore_signal(barrier, inc=1, device_id=(r, lax.rem(c + k, cols)), device_id_type=MESH)

    loop(1, rows, greet_row)
    loop(1, cols, greet_col)

    normed = unit_rows(feat[...])
    ncol[r] = normed
    nrow[c] = normed
    nnew[c] = unit_rows(feat_new[...])

    pl.semaphore_wait(barrier, rows + cols - 2)

    def spread_start(buf, send, recv):
        def to_pair(k):
            there = 2 * lax.rem(pair + k, half) + core
            remote(buf.at[r], buf.at[r], send.at[k], recv.at[r], there, c).start()

        loop(1, half, to_pair)
        remote(buf.at[r], buf.at[r], send.at[0], recv.at[r], mate, c).start()

    def like(k):
        return 2 * lax.rem(pair + half - k, half) + core

    def unlike(k):
        return 2 * lax.rem(pair + half - k, half) + 1 - core

    def spread_forward(buf, send, recv, use):
        def one(k):
            j = like(k)
            fwd = remote(buf.at[j], buf.at[j], send.at[half - 1 + k], recv.at[j], mate, c)
            fwd.wait_recv()
            fwd.start()
            use(j)

        loop(1, half, one)

    def spread_rest(buf, send, recv, use):
        def one(k):
            j = unlike(k)
            remote(buf.at[j], buf.at[j], send.at[0], recv.at[j], mate, c).wait_recv()
            use(j)

        loop(0, half, one)

    def spread_end(buf, send, recv):
        def one(k):
            remote(buf.at[r], buf.at[r], send.at[k], recv.at[r], mate, c).wait_send()

        loop(0, rows - 1, one)

    def line_start(src_of, dst, send, recv):
        def one(k):
            there = lax.rem(c + k, cols)
            remote(src_of(there), dst.at[c], send.at[k], recv.at[c], r, there).start()

        loop(1, cols, one)

    def line_wait(dst, send, recv, k):
        src = lax.rem(c + cols - k, cols)
        remote(dst.at[src], dst.at[src], send.at[k], recv.at[src], r, lax.rem(c + k, cols)).wait_recv()
        return src

    def line_end(dst, send, recv):
        def one(k):
            there = lax.rem(c + k, cols)
            remote(dst.at[c], dst.at[c], send.at[k], recv.at[c], r, there).wait_send()

        loop(1, cols, one)

    line_start(lambda there: nrow.at[c], nrow, z_send, z_recv)
    spread_start(ncol, n_send, n_recv)

    lane = lax.broadcasted_iota(jnp.int32, (points, width), 1)
    line = lax.broadcasted_iota(jnp.int32, (points, width), 0)
    repeat = (lax.rem(lane, points) == line).astype(F32)
    wide_row = lax.broadcasted_iota(jnp.int32, (width, width), 0) // points
    wide_col = lax.broadcasted_iota(jnp.int32, (width, width), 1) // points
    same = (wide_row == wide_col).astype(F32)
    mix_ref[...] = same * dot_full(repeat, dot_full(time_kernel[...], repeat), ((0,), (0,)))
    noise_cols = dot_full(jnp.broadcast_to(noise_var[...], (8, points)), repeat)[0:1]
    place = lax.rem(lax.broadcasted_iota(jnp.int32, (block, width), 1), points)
    mask = (place < lengths[...]).astype(F32)
    mask_ref[...] = mask
    rhs = mask * (dot_full(targets[...], repeat) - prior[...] - jnp.sqrt(noise_cols) * draw[...])
    rhs_ref[...] = rhs
    v0[r] = dot_full(rhs, mix_ref[...])
    spread_start(v0, v_send.at[0], v_recv.at[0])

    def keep_split(j):
        if keep:
            high, low = split(ncol[j])
            nch[j] = high
            ncl[j] = low

    def right(j):
        return (nch[j], ncl[j]) if keep else split(ncol[j])

    keep_split(r)
    spread_forward(ncol, n_send, n_recv, keep_split)
    spread_rest(ncol, n_send, n_recv, keep_split)

    def build(at):
        left = split(nrow[at])
        for j in range(rows):
            tile = cubic(dot3(left, right(j), NT))
            high, low = split(tile)
            kh[at, :, j * block : (j + 1) * block] = high
            kl[at, :, j * block : (j + 1) * block] = low

    build(c)

    def keep_values(j):
        high, low = split(v0[j])
        here = pl.ds(pl.multiple_of(j * block, block), block)
        vh[here, :] = high
        vl[here, :] = low

    keep_values(r)
    spread_forward(v0, v_send.at[0], v_recv.at[0], keep_values)

    def build_next(k):
        build(line_wait(nrow, z_send, z_recv, k))

    loop(1, cols, build_next)
    spread_rest(v0, v_send.at[0], v_recv.at[0], keep_values)

    relay = cols == 4
    if relay:
        end = 1 - lax.rem((c + 1) // 2, 2)
        near = 1 + c // 2
        edge = 3 * (c - 1)
        chunks = (3 - c, end * (3 - near) + (1 - end) * edge, end * near + (1 - end) * (3 - edge))
        to = (end * near + (1 - end) * (3 - c), chunks[1], chunks[2])
        slots = (end * near + (1 - end) * c, c, c)
    else:
        chunks = to = tuple(lax.rem(c + k, cols) for k in range(1, cols))
        slots = (c,) * (cols - 1)

    def chunk_copy(step, i):
        return remote(
            acc.at[chunks[i]], got.at[step, slots[i]], rs_send.at[step, i], rs_recv.at[step, slots[i]], r, to[i]
        )

    def arrival(step, src):
        return remote(got.at[step, src], got.at[step, src], rs_send.at[step, 0], rs_recv.at[step, src], mate, c)

    def apply(step):
        def product(there):
            acc[there] = dot3((kh[there], kl[there]), (vh[...], vl[...]), NN)

        for i in range(cols - 1):
            product(chunks[i])
            if relay and i == 2:

                @pl.when(end == 1)
                def _():
                    chunk_copy(step, i).start()

            else:
                chunk_copy(step, i).start()
        product(c)
        if relay:

            @pl.when(end == 0)
            def _():
                arrival(step, c).wait_recv()
                acc[chunks[2]] += got[step, c]
                chunk_copy(step, 2).start()

    def gathered(step):
        if relay:
            arrival(step, end + (1 - end) * (3 - c)).wait_recv()
            arrival(step, 2 * end).wait_recv()

            @pl.when(end == 0)
            def _():
                arrival(step, 3).wait_recv()

            @pl.when(end == 1)
            def _():
                got[step, 3 - c] = jnp.zeros(got.shape[2:], F32)

        else:
            for i in range(cols - 1):
                arrival(step, chunks[i]).wait_recv()
        got[step, c] = acc[c]
        return jnp.sum(got[step], axis=0)

    def chunks_end(step):
        for i in range(cols - 1):
            chunk_copy(step, i).wait_send()

    def cross(step):
        left = split(nnew[...].reshape(cols * fresh, nnew.shape[2]))
        xacc[step] = jnp.zeros(xacc.shape[1:], F32)

        def one(j):
            tile = split(cubic(dot3(left, right(j), NT)))
            here = pl.ds(pl.multiple_of(j * block, block), block)
            part = dot3(tile, (vh[here, :], vl[here, :]), NN)
            xacc[step] += part.reshape(cols, fresh, width)

        loop(0, rows, one)
        line_start(lambda there: xacc.at[step, there], xgot.at[step], xs_send.at[step], xs_recv.at[step])

    def reduced(dst, own, send, recv):
        def wait(k):
            line_wait(dst, send, recv, k)

        loop(1, cols, wait)
        dst[c] = own
        return jnp.sum(dst[...], axis=0)

    def total_start(step):
        def one(k):
            there = lax.rem(r + k, rows)
            remote(
                dots_row.at[step, r], dots_row.at[step, r], dr_send.at[step, k], dr_recv.at[step, r], there, c
            ).start()

        loop(1, rows, one)

    def total_middle(step):
        def one(k):
            j = lax.rem(r + rows - k, rows)
            remote(
                dots_row.at[step, j], dots_row.at[step, j], dr_send.at[step, k], dr_recv.at[step, j], mate, c
            ).wait_recv()

        loop(1, rows, one)
        dots_col[step, c] = jnp.sum(dots_row[step], axis=0)
        line_start(lambda there: dots_col.at[step, c], dots_col.at[step], dc_send.at[step], dc_recv.at[step])

    def total_end(step):
        def one(k):
            line_wait(dots_col.at[step], dc_send.at[step], dc_recv.at[step], k)

        loop(1, cols, one)
        return dot_full(jnp.sum(dots_col[step], axis=0), same)

    def total_close(step):
        def one(k):
            remote(
                dots_row.at[step, r], dots_row.at[step, r], dr_send.at[step, k], dr_recv.at[step, r], mate, c
            ).wait_send()

        loop(1, rows, one)
        line_end(dots_col.at[step], dc_send.at[step], dc_recv.at[step])

    def column_sums(*values):
        sums = [jnp.sum(v, axis=0, keepdims=True) for v in values]
        return jnp.concatenate(sums + [jnp.zeros((8 - len(sums), width), F32)], axis=0)

    acc = nrow
    line_end(nrow, z_send, z_recv)
    apply(0)
    line_start(lambda there: nnew.at[c], nnew, w_send, w_recv)

    def wait_new(k):
        line_wait(nnew, w_send, w_recv, k)

    image0 = mask_ref[...] * gathered(0) + noise_cols * rhs_ref[...]
    image_ref[...] = image0
    dots_row[0, r] = column_sums(rhs_ref[...] * rhs_ref[...], rhs_ref[...] * image0)
    total_start(0)
    v1[r] = dot_full(image0, mix_ref[...])
    spread_start(v1, v_send.at[1], v_recv.at[1])
    loop(1, cols, wait_new)
    total_middle(0)
    cross(0)
    sums0 = total_end(0)
    alpha0 = sums0[0:1] / sums0[1:2]

    def keep_next(j):
        high, low = split(v0[j] - alpha0 * v1[j])
        here = pl.ds(pl.multiple_of(j * block, block), block)
        vh[here, :] = high
        vl[here, :] = low

    keep_next(r)
    spread_forward(v1, v_send.at[1], v_recv.at[1], keep_next)

    chunks_end(0)
    spread_rest(v1, v_send.at[1], v_recv.at[1], keep_next)

    apply(1)
    cross(1)
    residual = rhs_ref[...] - alpha0 * image_ref[...]
    image1 = mask_ref[...] * gathered(1) + noise_cols * residual
    dots_row[1, r] = column_sums(
        residual * residual, residual * image1, residual * image_ref[...] + rhs_ref[...] * image1
    )
    total_start(1)
    total_middle(1)
    sums1 = total_end(1)
    ratio = sums1[0:1] / sums0[0:1]
    alpha1 = sums1[0:1] / (sums1[1:2] + ratio * (sums1[2:3] + ratio * sums0[1:2]))
    out_res[...] = residual - alpha1 * (image1 + ratio * image_ref[...])
    first = reduced(xgot.at[0], xacc[0, c], xs_send.at[0], xs_recv.at[0])
    second = reduced(xgot.at[1], xacc[1, c], xs_send.at[1], xs_recv.at[1])
    out_pred[...] = prior_new[...] + (alpha0 + alpha1 * ratio) * first + alpha1 * second

    spread_end(ncol, n_send, n_recv)
    line_end(nnew, w_send, w_recv)

    chunks_end(1)
    for step, buf in ((0, v0), (1, v1)):
        spread_end(buf, v_send.at[step], v_recv.at[step])
        line_end(xgot.at[step], xs_send.at[step], xs_recv.at[step])
        total_close(step)


def shards(rows, cols, features, new_features, lengths, targets, prior_train, noise_draw, prior_new, time_kernel, noise_var):
    block, depth = features.shape
    fresh = new_features.shape[0]
    width = prior_train.shape[1]
    vmem = pl.BlockSpec(memory_space=pltpu.VMEM)
    dma = pltpu.SemaphoreType.DMA
    assert depth == width
    keep = 4 * rows * cols * block * block <= 2**24
    kept = (rows, block, depth) if keep else (1, 16, depth)
    flops = 2 * 3 * block * cols * block * rows * (depth + 2 * width)
    return pl.pallas_call(
        functools.partial(body, rows, cols, keep),
        out_shape=(
            jax.ShapeDtypeStruct((block, width), F32),
            jax.ShapeDtypeStruct((fresh, width), F32),
        ),
        in_specs=[vmem] * 9,
        out_specs=(vmem, vmem),
        scratch_shapes=[
            pltpu.VMEM((rows, block, depth), F32),
            pltpu.VMEM((cols, block, depth), F32),
            pltpu.VMEM((cols, fresh, depth), F32),
            pltpu.VMEM((rows, block, width), F32),
            pltpu.VMEM((rows, block, width), F32),
            pltpu.VMEM(kept, BF16),
            pltpu.VMEM(kept, BF16),
            pltpu.VMEM((cols, block, rows * block), BF16),
            pltpu.VMEM((cols, block, rows * block), BF16),
            pltpu.VMEM((rows * block, width), BF16),
            pltpu.VMEM((rows * block, width), BF16),
            pltpu.VMEM((2, cols, fresh, width), F32),
            pltpu.VMEM((2, cols, block, width), F32),
            pltpu.VMEM((2, cols, fresh, width), F32),
            pltpu.VMEM((block, width), F32),
            pltpu.VMEM((block, width), F32),
            pltpu.VMEM((block, width), F32),
            pltpu.VMEM((width, width), F32),
            pltpu.VMEM((2, rows, 8, width), F32),
            pltpu.VMEM((2, cols, 8, width), F32),
            dma((rows,)),
            dma((rows,)),
            dma((2, rows)),
            dma((2, rows)),
            dma((cols,)),
            dma((cols,)),
            dma((cols,)),
            dma((cols,)),
            dma((2, cols)),
            dma((2, cols)),
            dma((2, cols)),
            dma((2, cols)),
            dma((2, rows)),
            dma((2, rows)),
            dma((2, cols)),
            dma((2, cols)),
        ],
        compiler_params=pltpu.CompilerParams(
            collective_id=0, has_side_effects=True, vmem_limit_bytes=63 * 2**20
        ),
        cost_estimate=pl.CostEstimate(flops=flops, bytes_accessed=8 * block * width * 4, transcendentals=0),
    )(
        features,
        new_features,
        lengths.reshape(block, 1),
        targets,
        prior_train,
        noise_draw,
        prior_new,
        time_kernel,
        noise_var.reshape(1, -1),
    )


def solution(mesh):
    both = ("row", "col")
    return jax.shard_map(
        functools.partial(shards, mesh.shape["row"], mesh.shape["col"]),
        mesh=mesh,
        in_specs=(
            P(both, None),
            P(both, None),
            P(both),
            P(both, None),
            P(both, None),
            P(both, None),
            P(both, None),
            P(),
            P(),
        ),
        out_specs=(P(both, None), P(both, None)),
        check_vma=False,
    )
```
